32 devices in a mesh: member: 4 (over y, x), fsdp: 8 (over z, core).
Axes of the slice: x: 2, y: 2, z: 4, core: 2. Of those that a mesh axis runs over, the one named last changes fastest.
Arguments:
- tokens: bfloat16 [4, 1024, 2048], P('member', 'fsdp'), may hold values from -6 to 6
- out_grad: bfloat16 [4, 1024, 8192], P('member', 'fsdp'), may hold values from -2 to 2
- master: float32 [4, 2048, 8192], P('member', None, 'fsdp'), may hold values from -0.125 to 0.125
- first_moment: bfloat16 [4, 2048, 8192], P('member', None, 'fsdp'), may hold values from -6 to 6
- second_moment: bfloat16 [4, 2048, 8192], P('member', None, 'fsdp'), may hold values from 1 to 100
- source: int32 [4], replicated, may hold values from 0 to 3, as said below
- perturb: int32 [4], replicated, may hold values from 0 to 3
Outputs:
- new_master: float32 [4, 2048, 8192], P('member', None, 'fsdp')
- new_first: bfloat16 [4, 2048, 8192], P('member', None, 'fsdp')
- new_second: bfloat16 [4, 2048, 8192], P('member', None, 'fsdp')
- gate_out: bfloat16 [4, 1024, 8192], P('member', None, 'fsdp')
The draws below stay inside these ranges and needn't reach their ends.
Inputs may be any that keep to these rules, and one draw needn't show every extreme that they name: Exactly 1 members i have source[i] != i; every member named as a source has its own index as source.
All inputs are finite; a program needn't handle non-finite values.
Results may differ from the reference program's by a relative error of at most 0.0049.
Values may be sent and summed in bfloat16 or wider, within the bound.
A program may use at most 128 MiB of HBM per device.

```python
import math
import jax
import jax.numpy as jnp
from jax import lax

D = 2048
FF = 8192
MEMBERS = 4
LOSERS = 1
TOKENS = 1024


def draw_source(key, part):
    keys = jax.random.split(key, 2)
    scores = jax.random.randint(keys[0], (MEMBERS,), 0, 1048576).astype(jnp.int32)
    scores = scores * MEMBERS + jnp.arange(MEMBERS, dtype=jnp.int32)
    order = jnp.argsort(scores, stable=True).astype(jnp.int32)
    picks = jax.random.randint(keys[1], (LOSERS,), LOSERS, MEMBERS).astype(jnp.int32)
    result = jnp.arange(MEMBERS, dtype=jnp.int32)
    return result.at[order[:LOSERS]].set(order[picks])


def touch_ends(values, own_key, least, top_value):
    longest = values.shape.index(max(values.shape))
    spots = []
    for shift in (0, 1):
        where = [jax.random.randint(jax.random.fold_in(own_key, axis), (), 0, length) for axis, length in enumerate(values.shape)]
        where[longest] = (where[longest] + shift) % values.shape[longest]
        spots.append(tuple(where))
    return values.at[spots[0]].set(least).at[spots[1]].set(top_value)


def level_of(rng, shape, cuts, low, high):
    def one(dim, shards_of):
        heights = jax.random.uniform(jax.random.fold_in(jax.random.fold_in(rng, 6), dim), (shards_of,), jnp.float32, low / len(cuts), high / len(cuts))
        return jnp.repeat(jnp.exp(heights), shape[dim] // shards_of).reshape((-1,) + (1,) * (len(shape) - dim - 1))

    level = one(*cuts[0])
    for cut in cuts[1:]:
        level = level * one(*cut)
    return level


def normal_values(rng, dims, width, reach, cuts=(), kind=jnp.bfloat16):
    values = width * jax.random.normal(rng, dims, jnp.float32)
    if cuts:
        values = values * level_of(rng, dims, cuts, -0.22, 0.18)
    return jnp.clip(values, -reach, reach).astype(kind)


def setup_inputs(seed: int = 0) -> dict:
    splits = jax.random.split(jax.random.key(seed), 8)
    tokens = normal_values(splits[0], (MEMBERS, TOKENS, D), 1.0, 6.0, ((0, 4), (1, 8)))
    out_grad = normal_values(splits[1], (MEMBERS, TOKENS, FF), 0.15, 2.0, ((0, 4), (1, 8)))
    master = normal_values(splits[2], (MEMBERS, D, FF), D ** -0.5, 0.125, ((0, 4), (2, 8)), jnp.float32)
    first_moment = normal_values(splits[3], (MEMBERS, D, FF), 1.0, 6.0, ((0, 4), (2, 8)))
    second_moment = jnp.clip(jnp.exp(math.log(100.0) - 4.6051702 * jax.random.uniform(splits[4], (MEMBERS, D, FF), jnp.float32) ** level_of(splits[4], (MEMBERS, D, FF), ((0, 4), (2, 8)), -0.2, 0.2)), 1.0, 100.0).astype(jnp.bfloat16)
    source = draw_source(jax.random.fold_in(splits[7], 71), 0)
    perturb = touch_ends(jax.random.randint(splits[6], (MEMBERS,), 0, 4), jax.random.fold_in(splits[6], 1), 0, 3).astype(jnp.int32)
    return dict(tokens=tokens, out_grad=out_grad, master=master, first_moment=first_moment, second_moment=second_moment, source=source, perturb=perturb)


rate_factors = (0.5, 0.8, 1.25, 2.0)
base_rate = 0.02
decay = 0.1
epsilon = 1e-08

def reference(tokens, out_grad, master, first_moment, second_moment, source, perturb):
    table = jnp.array(rate_factors, dtype=jnp.float32)

    def member_step(index):
        anchor = source[index]
        weight = master[anchor]
        first_old = first_moment[anchor].astype(jnp.float32)
        second_old = second_moment[anchor].astype(jnp.float32)
        inputs = tokens[index]
        grad = jnp.dot(inputs.T, out_grad[index], preferred_element_type=jnp.float32)
        first = 0.9 * first_old + 0.1 * grad
        second = 0.95 * second_old + 0.05 * grad * grad
        rate = base_rate * table[perturb[index]]
        updated = weight - rate * (first / (jnp.sqrt(second) + epsilon) + decay * weight)
        weight_half = updated.astype(jnp.bfloat16)
        gate_out = jnp.dot(inputs, weight_half, preferred_element_type=jnp.float32).astype(jnp.bfloat16)
        return (updated, first.astype(jnp.bfloat16), second.astype(jnp.bfloat16), gate_out)
    outputs = lax.map(member_step, jnp.arange(MEMBERS, dtype=jnp.int32))
    return (outputs[0], outputs[1], outputs[2], outputs[3])
```

```python
import functools
import jax
import jax.numpy as jnp
from jax import lax
from jax.experimental import pallas as pl
from jax.experimental.pallas import tpu as pltpu
from jax.sharding import PartitionSpec as P

rate_factors = (0.5, 0.8, 1.25, 2.0)
base_rate = 0.02
decay = 0.1
epsilon = 1e-08
MESH = pl.DeviceIdType.MESH
MIB = 1024 * 1024


def routes(loser, anchor):
    apart = loser ^ anchor
    if apart == 3:
        return [(anchor, anchor ^ 1, loser), (anchor, anchor ^ 2, loser)]
    other = 3 - apart
    return [(anchor, loser), (anchor, anchor ^ other, loser ^ other, loser)]


def exchange_kernel(
    loser, anchor, chunk,
    tokens, out_grad, master, first, second,
    gathered, cols, got_master, got_first, got_second,
    wide, narrow, token_send, token_recv, grad_send, grad_recv,
    state_send, state_recv, local_sem,
):
    members = lax.axis_size("member")
    ring = lax.axis_size("fsdp")
    mine = lax.axis_index("fsdp")
    member = lax.axis_index("member")
    rows = tokens.shape[1]
    width = cols.shape[1]

    barrier = pltpu.get_barrier_semaphore()
    for step in range(1, ring):
        pl.semaphore_signal(
            barrier, inc=1, device_id={"fsdp": lax.rem(mine + step, ring)}, device_id_type=MESH
        )
    for step in range(1, members):
        pl.semaphore_signal(
            barrier, inc=1, device_id={"member": lax.rem(member + step, members)}, device_id_type=MESH
        )
    pl.semaphore_wait(barrier, ring + members - 2)

    ways = routes(loser, anchor)
    depth = master.shape[1]
    pieces = depth // chunk
    split = pieces // 2 if len(ways[0]) == len(ways[1]) else pieces // 2 + pieces // 32
    spans = ((0, split), (split, pieces))
    landing = (got_first, got_second, got_master)
    starting = (first.at[0], second.at[0], narrow)

    def state_copy(kind, piece, origin, target):
        at = pl.ds(pl.multiple_of(piece * chunk, chunk), chunk)
        return pltpu.make_async_remote_copy(
            src_ref=(starting if origin else landing)[kind].at[at],
            dst_ref=landing[kind].at[at],
            send_sem=state_send.at[kind, piece],
            recv_sem=state_recv.at[kind, piece],
            device_id={"member": target},
            device_id_type=MESH,
        )

    load = pltpu.make_async_copy(master.at[0], wide, local_sem.at[0])

    @pl.when(member == anchor)
    def _():
        load.start()
        for kind in (0, 1):
            for way, (low, high) in reversed(tuple(zip(ways, spans))):
                @pl.loop(low, high)
                def _(piece):
                    state_copy(kind, piece, True, way[1]).start()

    my_rows = pl.ds(pl.multiple_of(mine * rows, rows), rows)

    def token_copy(step):
        return pltpu.make_async_remote_copy(
            src_ref=tokens.at[0],
            dst_ref=gathered.at[my_rows],
            send_sem=token_send.at[step],
            recv_sem=token_recv.at[step],
            device_id={"fsdp": lax.rem(mine + step, ring)},
            device_id_type=MESH,
        )

    def grad_copy(step):
        target = lax.rem(mine + step, ring)
        return pltpu.make_async_remote_copy(
            src_ref=out_grad.at[0, :, pl.ds(pl.multiple_of(target * width, width), width)],
            dst_ref=cols.at[my_rows],
            send_sem=grad_send.at[step],
            recv_sem=grad_recv.at[step],
            device_id={"fsdp": target},
            device_id_type=MESH,
        )

    for step in range(1, ring):
        grad_copy(step).start()
        token_copy(step).start()
    own_tokens = pltpu.make_async_copy(tokens.at[0], gathered.at[my_rows], local_sem.at[1])
    own_grad = pltpu.make_async_copy(
        out_grad.at[0, :, pl.ds(pl.multiple_of(mine * width, width), width)],
        cols.at[my_rows],
        local_sem.at[2],
    )
    own_tokens.start()
    own_grad.start()

    @pl.when(member == anchor)
    def _():
        load.wait()
        for way, (low, high) in reversed(tuple(zip(ways, spans))):
            @pl.loop(low, high)
            def _(piece):
                at = pl.ds(pl.multiple_of(piece * chunk, chunk), chunk)
                narrow[at, :] = wide[at, :].astype(narrow.dtype)
                state_copy(2, piece, True, way[1]).start()

    for way, (low, high) in zip(ways, spans):
        for here in range(1, len(way) - 1):
            @pl.when(member == way[here])
            def _():
                for kind in range(3):
                    @pl.loop(low, high)
                    def _(piece):
                        passed = state_copy(kind, piece, False, way[here + 1])
                        passed.wait_recv()
                        passed.start()

    for step in range(1, ring):
        grad_copy(step).wait()
        token_copy(step).wait()
    own_tokens.wait()
    own_grad.wait()

    for way, (low, high) in zip(ways, spans):
        @pl.when(member == way[-1])
        def _():
            for kind in range(3):
                @pl.loop(low, high)
                def _(piece):
                    state_copy(kind, piece, False, way[-2]).wait_recv()

        for here in range(len(way) - 1):
            @pl.when(member == way[here])
            def _():
                for kind in range(3):
                    @pl.loop(low, high)
                    def _(piece):
                        state_copy(kind, piece, here == 0, way[here + 1]).wait_send()


def exchange(loser, anchor, number, tokens, out_grad, master, first, second):
    ring = lax.axis_size("fsdp")
    _, rows, depth = tokens.shape
    width = master.shape[2]
    chunk = 64
    pieces = depth // chunk
    half = jax.ShapeDtypeStruct((depth, width), jnp.bfloat16)
    spot = pl.BlockSpec(memory_space=pl.ANY)
    return pl.pallas_call(
        functools.partial(exchange_kernel, loser, anchor, chunk),
        out_shape=(
            jax.ShapeDtypeStruct((ring * rows, depth), tokens.dtype),
            jax.ShapeDtypeStruct((ring * rows, width), out_grad.dtype),
            half,
            half,
            half,
        ),
        in_specs=[spot] * 5,
        out_specs=[spot] * 5,
        scratch_shapes=[
            pltpu.VMEM((depth, width), jnp.float32),
            pltpu.VMEM((depth, width), jnp.bfloat16),
            pltpu.SemaphoreType.DMA((ring,)),
            pltpu.SemaphoreType.DMA((ring,)),
            pltpu.SemaphoreType.DMA((ring,)),
            pltpu.SemaphoreType.DMA((ring,)),
            pltpu.SemaphoreType.DMA((3, pieces)),
            pltpu.SemaphoreType.DMA((3, pieces)),
            pltpu.SemaphoreType.DMA((3,)),
        ],
        compiler_params=pltpu.CompilerParams(
            collective_id=number, has_side_effects=True, vmem_limit_bytes=40 * MIB
        ),
    )(tokens, out_grad, master, first, second)


def update_kernel(
    taken, rate_ref, inputs, cols, own_master, own_first, own_second, got_master, got_first, got_second,
    new_master, new_first, new_second, gate_out, total,
):
    step = pl.program_id(0)
    is_taken = taken[0] == 1
    rate = rate_ref[0]
    block = inputs[...]
    grad = lax.dot_general(
        block, cols[...], (((0,), (0,)), ((), ())), preferred_element_type=jnp.float32
    )
    weight = jnp.where(is_taken, got_master[...].astype(jnp.float32), own_master[0])
    first_old = jnp.where(is_taken, got_first[...], own_first[0]).astype(jnp.float32)
    second_old = jnp.where(is_taken, got_second[...], own_second[0]).astype(jnp.float32)
    first = 0.9 * first_old + 0.1 * grad
    second = 0.95 * second_old + 0.05 * grad * grad
    updated = weight - rate * (first / (jnp.sqrt(second) + epsilon) + decay * weight)
    new_master[0] = updated
    new_first[0] = first.astype(jnp.bfloat16)
    new_second[0] = second.astype(jnp.bfloat16)
    part = jnp.dot(block, updated.astype(jnp.bfloat16), preferred_element_type=jnp.float32)

    @pl.when(step == 0)
    def _():
        total[...] = part

    @pl.when(step > 0)
    def _():
        total[...] += part

    @pl.when(step == pl.num_programs(0) - 1)
    def _():
        gate_out[0] = total[...].astype(jnp.bfloat16)


def update(taken, rate, gathered, cols, master, first, second, got_master, got_first, got_second):
    count, depth = gathered.shape
    width = cols.shape[1]
    block = 256

    own = pl.BlockSpec((1, block, width), lambda i, t, r: (0, i * (1 - t[0]), 0))
    got = pl.BlockSpec((block, width), lambda i, t, r: (i * t[0], 0))
    new = pl.BlockSpec((1, block, width), lambda i, t, r: (0, i, 0))
    return pl.pallas_call(
        update_kernel,
        out_shape=(
            jax.ShapeDtypeStruct((1, depth, width), jnp.float32),
            jax.ShapeDtypeStruct((1, depth, width), jnp.bfloat16),
            jax.ShapeDtypeStruct((1, depth, width), jnp.bfloat16),
            jax.ShapeDtypeStruct((1, count, width), jnp.bfloat16),
        ),
        grid_spec=pltpu.PrefetchScalarGridSpec(
            num_scalar_prefetch=2,
            grid=(depth // block,),
            in_specs=[
                pl.BlockSpec((count, block), lambda i, t, r: (0, i)),
                pl.BlockSpec((count, width), lambda i, t, r: (0, 0)),
                own, own, own, got, got, got,
            ],
            out_specs=[
                new, new, new,
                pl.BlockSpec((1, count, width), lambda i, t, r: (0, 0, 0)),
            ],
            scratch_shapes=[pltpu.VMEM((count, width), jnp.float32)],
        ),
        compiler_params=pltpu.CompilerParams(vmem_limit_bytes=52 * MIB),
    )(taken, rate, gathered, cols, master, first, second, got_master, got_first, got_second)


def rate_of(perturb, member_index, positions):
    my_level = jnp.sum(jnp.where(positions == member_index, perturb, 0))
    table = jnp.array(rate_factors, dtype=jnp.float32)
    levels = jnp.arange(len(rate_factors), dtype=jnp.int32)
    return base_rate * jnp.sum(jnp.where(levels == my_level, table, 0.0))


def square_shards(tokens, out_grad, master, first_moment, second_moment, source, perturb):
    count = lax.axis_size("member")
    member_index = lax.axis_index("member")
    positions = jnp.arange(count, dtype=jnp.int32)
    loser = jnp.sum(jnp.where(source != positions, positions, 0))
    anchor = jnp.sum(jnp.where(positions == loser, source, 0))
    pairs = [(i, j) for i in range(count) for j in range(count) if i != j]
    branch = sum(jnp.where((loser == i) & (anchor == j), k, 0) for k, (i, j) in enumerate(pairs))
    got = lax.switch(
        branch,
        [functools.partial(exchange, i, j, k) for k, (i, j) in enumerate(pairs)],
        tokens, out_grad, master, first_moment, second_moment,
    )
    gathered, cols, got_master, got_first, got_second = got
    rate = rate_of(perturb, member_index, positions)
    taken = ((member_index == loser) & (loser != anchor)).astype(jnp.int32)
    return update(
        taken[None], rate[None], gathered, cols, master, first_moment, second_moment,
        got_master, got_first, got_second,
    )


def from_root(value, axis, source):
    kept = jnp.where(lax.axis_index(axis) == source, value, 0).astype(value.dtype)
    return lax.psum(kept, axis)


def general_shards(tokens, out_grad, master, first_moment, second_moment, source, perturb):
    count = lax.axis_size("member")
    member_index = lax.axis_index("member")
    positions = jnp.arange(count, dtype=jnp.int32)
    moments = jnp.stack([first_moment, second_moment], 1)
    losers_total = 3 * count // 8
    copying = source != positions
    earlier = positions[None, :] < positions[:, None]
    rank = jnp.sum(jnp.where(earlier & copying[None, :], 1, 0), axis=1)
    master_now = master
    moments_now = moments
    for turn in range(losers_total):
        target = jnp.sum(jnp.where(copying & (rank == turn), positions, 0))
        anchor = jnp.sum(jnp.where(positions == target, source, 0))
        got_master = from_root(master, "member", anchor)
        got_moments = from_root(moments, "member", anchor)
        taken = member_index == target
        master_now = jnp.where(taken, got_master, master_now)
        moments_now = jnp.where(taken, got_moments, moments_now)
    gathered = lax.all_gather(tokens, "fsdp", axis=1, tiled=True)
    grad_cols = lax.all_to_all(out_grad, "fsdp", split_axis=2, concat_axis=1, tiled=True)
    inputs = gathered[0]
    grad = lax.dot_general(
        inputs, grad_cols[0], (((0,), (0,)), ((), ())), preferred_element_type=jnp.float32
    )
    first = 0.9 * moments_now[0, 0].astype(jnp.float32) + 0.1 * grad
    second = 0.95 * moments_now[0, 1].astype(jnp.float32) + 0.05 * grad * grad
    rate = rate_of(perturb, member_index, positions)
    weight = master_now[0]
    updated = weight - rate * (first / (jnp.sqrt(second) + epsilon) + decay * weight)
    weight_half = updated.astype(jnp.bfloat16)
    gate_out = jnp.dot(inputs, weight_half, preferred_element_type=jnp.float32).astype(jnp.bfloat16)
    return (
        updated[None],
        first.astype(jnp.bfloat16)[None],
        second.astype(jnp.bfloat16)[None],
        gate_out[None],
    )


def solution(mesh):
    in_specs = (
        P("member", "fsdp", None),
        P("member", "fsdp", None),
        P("member", None, "fsdp"),
        P("member", None, "fsdp"),
        P("member", None, "fsdp"),
        P(),
        P(),
    )
    out_specs = (
        P("member", None, "fsdp"),
        P("member", None, "fsdp"),
        P("member", None, "fsdp"),
        P("member", None, "fsdp"),
    )
    shards = square_shards if mesh.shape["member"] == 4 else general_shards
    return jax.shard_map(shards, mesh=mesh, in_specs=in_specs, out_specs=out_specs, check_vma=False)
```

```python
import functools
import jax
import numpy as np
import jax.numpy as jnp
from jax import lax
from jax.experimental import pallas as pl
from jax.experimental.pallas import tpu as pltpu
from jax.sharding import PartitionSpec as P

rate_factors = (0.5, 0.8, 1.25, 2.0)
base_rate = 0.02
decay = 0.1
epsilon = 1e-08
MESH = pl.DeviceIdType.MESH
MIB = 1024 * 1024


def routes(loser, anchor):
    apart = loser ^ anchor
    if apart == 3:
        return [(anchor, anchor ^ 1, loser), (anchor, anchor ^ 2, loser)]
    other = 3 - apart
    return [(anchor, loser), (anchor, anchor ^ other, loser ^ other, loser)]


def exchange_kernel(
    loser, anchor, chunk,
    tokens, out_grad, master, first, second,
    gathered, cols, got_master, got_first, got_second,
    wide, narrow, token_send, token_recv, grad_send, grad_recv,
    state_send, state_recv, local_sem,
):
    members = lax.axis_size("member")
    ring = lax.axis_size("fsdp")
    mine = lax.axis_index("fsdp")
    member = lax.axis_index("member")
    rows = tokens.shape[1]
    width = cols.shape[1]

    barrier = pltpu.get_barrier_semaphore()
    for step in range(1, ring):
        pl.semaphore_signal(
            barrier, inc=1, device_id={"fsdp": lax.rem(mine + step, ring)}, device_id_type=MESH
        )
    for step in range(1, members):
        pl.semaphore_signal(
            barrier, inc=1, device_id={"member": lax.rem(member + step, members)}, device_id_type=MESH
        )
    pl.semaphore_wait(barrier, ring + members - 2)

    ways = routes(loser, anchor)
    depth = master.shape[1]
    pieces = depth // chunk
    split = pieces // 2 if len(ways[0]) == len(ways[1]) else pieces // 2 + 1
    spans = ((0, split), (split, pieces))
    landing = (got_first, got_second, got_master)
    starting = (first.at[0], second.at[0], narrow)

    def state_copy(kind, piece, origin, target):
        at = pl.ds(pl.multiple_of(piece * chunk, chunk), chunk)
        return pltpu.make_async_remote_copy(
            src_ref=(starting if origin else landing)[kind].at[at],
            dst_ref=landing[kind].at[at],
            send_sem=state_send.at[kind, piece],
            recv_sem=state_recv.at[kind, piece],
            device_id={"member": target},
            device_id_type=MESH,
        )

    load = pltpu.make_async_copy(master.at[0], wide, local_sem.at[0])

    @pl.when(member == anchor)
    def _():
        load.start()
        for kind in (0, 1):
            for way, (low, high) in reversed(tuple(zip(ways, spans))):
                @pl.loop(low, high)
                def _(piece):
                    state_copy(kind, piece, True, way[1]).start()

    my_rows = pl.ds(pl.multiple_of(mine * rows, rows), rows)

    def token_copy(step):
        return pltpu.make_async_remote_copy(
            src_ref=tokens.at[0],
            dst_ref=gathered.at[my_rows],
            send_sem=token_send.at[step],
            recv_sem=token_recv.at[step],
            device_id={"fsdp": lax.rem(mine + step, ring)},
            device_id_type=MESH,
        )

    def grad_copy(step):
        target = lax.rem(mine + step, ring)
        return pltpu.make_async_remote_copy(
            src_ref=out_grad.at[0, :, pl.ds(pl.multiple_of(target * width, width), width)],
            dst_ref=cols.at[my_rows],
            send_sem=grad_send.at[step],
            recv_sem=grad_recv.at[step],
            device_id={"fsdp": target},
            device_id_type=MESH,
        )

    for step in range(1, ring):
        grad_copy(step).start()
        token_copy(step).start()
    own_tokens = pltpu.make_async_copy(tokens.at[0], gathered.at[my_rows], local_sem.at[1])
    own_grad = pltpu.make_async_copy(
        out_grad.at[0, :, pl.ds(pl.multiple_of(mine * width, width), width)],
        cols.at[my_rows],
        local_sem.at[2],
    )
    own_tokens.start()
    own_grad.start()

    @pl.when(member == anchor)
    def _():
        load.wait()
        for way, (low, high) in reversed(tuple(zip(ways, spans))):
            @pl.loop(low, high)
            def _(piece):
                at = pl.ds(pl.multiple_of(piece * chunk, chunk), chunk)
                narrow[at, :] = wide[at, :].astype(narrow.dtype)
                state_copy(2, piece, True, way[1]).start()

    for way, (low, high) in zip(ways, spans):
        for here in range(1, len(way) - 1):
            @pl.when(member == way[here])
            def _():
                for kind in range(3):
                    @pl.loop(low, high)
                    def _(piece):
                        passed = state_copy(kind, piece, False, way[here + 1])
                        passed.wait_recv()
                        passed.start()

    for step in range(1, ring):
        grad_copy(step).wait()
        token_copy(step).wait()
    own_tokens.wait()
    own_grad.wait()

    for way, (low, high) in zip(ways, spans):
        @pl.when(member == way[-1])
        def _():
            for kind in range(3):
                @pl.loop(low, high)
                def _(piece):
                    state_copy(kind, piece, False, way[-2]).wait_recv()

        for here in range(len(way) - 1):
            @pl.when(member == way[here])
            def _():
                for kind in range(3):
                    @pl.loop(low, high)
                    def _(piece):
                        state_copy(kind, piece, here == 0, way[here + 1]).wait_send()


def exchange(loser, anchor, number, tokens, out_grad, master, first, second):
    ring = lax.axis_size("fsdp")
    _, rows, depth = tokens.shape
    width = master.shape[2]
    chunk = 32
    pieces = depth // chunk
    half = jax.ShapeDtypeStruct((depth, width), jnp.bfloat16)
    spot = pl.BlockSpec(memory_space=pl.ANY)
    return pl.pallas_call(
        functools.partial(exchange_kernel, loser, anchor, chunk),
        out_shape=(
            jax.ShapeDtypeStruct((ring * rows, depth), tokens.dtype),
            jax.ShapeDtypeStruct((ring * rows, width), out_grad.dtype),
            half,
            half,
            half,
        ),
        in_specs=[spot] * 5,
        out_specs=[spot] * 5,
        scratch_shapes=[
            pltpu.VMEM((depth, width), jnp.float32),
            pltpu.VMEM((depth, width), jnp.bfloat16),
            pltpu.SemaphoreType.DMA((ring,)),
            pltpu.SemaphoreType.DMA((ring,)),
            pltpu.SemaphoreType.DMA((ring,)),
            pltpu.SemaphoreType.DMA((ring,)),
            pltpu.SemaphoreType.DMA((3, pieces)),
            pltpu.SemaphoreType.DMA((3, pieces)),
            pltpu.SemaphoreType.DMA((3,)),
        ],
        compiler_params=pltpu.CompilerParams(
            collective_id=number, has_side_effects=True, vmem_limit_bytes=40 * MIB
        ),
    )(tokens, out_grad, master, first, second)


def update_kernel(
    source, perturb, place, inputs, cols, own_master, own_first, own_second, got_master, got_first, got_second,
    new_master, new_first, new_second, gate_out, total,
):
    step = pl.program_id(0)
    is_taken = source[place[0]] != place[0]
    level = perturb[place[0]]
    rate = jnp.float32(0.0)
    for index, factor in enumerate(rate_factors):
        rate = jnp.where(level == index, np.float32(base_rate) * np.float32(factor), rate)
    block = inputs[...]
    grad = lax.dot_general(
        block, cols[...], (((0,), (0,)), ((), ())), preferred_element_type=jnp.float32
    )
    weight = jnp.where(is_taken, got_master[...].astype(jnp.float32), own_master[0])
    first_old = jnp.where(is_taken, got_first[...], own_first[0]).astype(jnp.float32)
    second_old = jnp.where(is_taken, got_second[...], own_second[0]).astype(jnp.float32)
    first = 0.9 * first_old + 0.1 * grad
    second = 0.95 * second_old + 0.05 * grad * grad
    updated = weight - rate * (first / (jnp.sqrt(second) + epsilon) + decay * weight)
    new_master[0] = updated
    new_first[0] = first.astype(jnp.bfloat16)
    new_second[0] = second.astype(jnp.bfloat16)
    part = jnp.dot(block, updated.astype(jnp.bfloat16), preferred_element_type=jnp.float32)

    @pl.when(step == 0)
    def _():
        total[...] = part

    @pl.when(step > 0)
    def _():
        total[...] += part

    @pl.when(step == pl.num_programs(0) - 1)
    def _():
        gate_out[0] = total[...].astype(jnp.bfloat16)


def update(source, perturb, place, gathered, cols, master, first, second, got_master, got_first, got_second):
    count, depth = gathered.shape
    width = cols.shape[1]
    block = 256

    own = pl.BlockSpec(
        (1, block, width), lambda i, s, p, m: (0, jnp.where(s[m[0]] == m[0], i, 0), 0)
    )
    got = pl.BlockSpec((block, width), lambda i, s, p, m: (jnp.where(s[m[0]] == m[0], 0, i), 0))
    new = pl.BlockSpec((1, block, width), lambda i, s, p, m: (0, i, 0))
    return pl.pallas_call(
        update_kernel,
        out_shape=(
            jax.ShapeDtypeStruct((1, depth, width), jnp.float32),
            jax.ShapeDtypeStruct((1, depth, width), jnp.bfloat16),
            jax.ShapeDtypeStruct((1, depth, width), jnp.bfloat16),
            jax.ShapeDtypeStruct((1, count, width), jnp.bfloat16),
        ),
        grid_spec=pltpu.PrefetchScalarGridSpec(
            num_scalar_prefetch=3,
            grid=(depth // block,),
            in_specs=[
                pl.BlockSpec((count, block), lambda i, s, p, m: (0, i)),
                pl.BlockSpec((count, width), lambda i, s, p, m: (0, 0)),
                own, own, own, got, got, got,
            ],
            out_specs=[
                new, new, new,
                pl.BlockSpec((1, count, width), lambda i, s, p, m: (0, 0, 0)),
            ],
            scratch_shapes=[pltpu.VMEM((count, width), jnp.float32)],
        ),
        compiler_params=pltpu.CompilerParams(vmem_limit_bytes=52 * MIB),
    )(source, perturb, place, gathered, cols, master, first, second, got_master, got_first, got_second)


def rate_of(perturb, member_index, positions):
    my_level = jnp.sum(jnp.where(positions == member_index, perturb, 0))
    table = jnp.array(rate_factors, dtype=jnp.float32)
    levels = jnp.arange(len(rate_factors), dtype=jnp.int32)
    return base_rate * jnp.sum(jnp.where(levels == my_level, table, 0.0))


def square_shards(tokens, out_grad, master, first_moment, second_moment, source, perturb):
    count = lax.axis_size("member")
    member_index = lax.axis_index("member")
    positions = jnp.arange(count, dtype=jnp.int32)
    pairs = [(i, j) for i in range(count) for j in range(count) if i != j]
    order = positions * (count - 1) + source - (source > positions).astype(jnp.int32)
    branch = jnp.sum(jnp.where(source != positions, order, 0))
    got = lax.switch(
        branch,
        [functools.partial(exchange, i, j, k) for k, (i, j) in enumerate(pairs)],
        tokens, out_grad, master, first_moment, second_moment,
    )
    gathered, cols, got_master, got_first, got_second = got
    return update(
        source, perturb, member_index[None], gathered, cols, master, first_moment, second_moment,
        got_master, got_first, got_second,
    )


def from_root(value, axis, source):
    kept = jnp.where(lax.axis_index(axis) == source, value, 0).astype(value.dtype)
    return lax.psum(kept, axis)


def general_shards(tokens, out_grad, master, first_moment, second_moment, source, perturb):
    count = lax.axis_size("member")
    member_index = lax.axis_index("member")
    positions = jnp.arange(count, dtype=jnp.int32)
    moments = jnp.stack([first_moment, second_moment], 1)
    losers_total = 3 * count // 8
    copying = source != positions
    earlier = positions[None, :] < positions[:, None]
    rank = jnp.sum(jnp.where(earlier & copying[None, :], 1, 0), axis=1)
    master_now = master
    moments_now = moments
    for turn in range(losers_total):
        target = jnp.sum(jnp.where(copying & (rank == turn), positions, 0))
        anchor = jnp.sum(jnp.where(positions == target, source, 0))
        got_master = from_root(master, "member", anchor)
        got_moments = from_root(moments, "member", anchor)
        taken = member_index == target
        master_now = jnp.where(taken, got_master, master_now)
        moments_now = jnp.where(taken, got_moments, moments_now)
    gathered = lax.all_gather(tokens, "fsdp", axis=1, tiled=True)
    grad_cols = lax.all_to_all(out_grad, "fsdp", split_axis=2, concat_axis=1, tiled=True)
    inputs = gathered[0]
    grad = lax.dot_general(
        inputs, grad_cols[0], (((0,), (0,)), ((), ())), preferred_element_type=jnp.float32
    )
    first = 0.9 * moments_now[0, 0].astype(jnp.float32) + 0.1 * grad
    second = 0.95 * moments_now[0, 1].astype(jnp.float32) + 0.05 * grad * grad
    rate = rate_of(perturb, member_index, positions)
    weight = master_now[0]
    updated = weight - rate * (first / (jnp.sqrt(second) + epsilon) + decay * weight)
    weight_half = updated.astype(jnp.bfloat16)
    gate_out = jnp.dot(inputs, weight_half, preferred_element_type=jnp.float32).astype(jnp.bfloat16)
    return (
        updated[None],
        first.astype(jnp.bfloat16)[None],
        second.astype(jnp.bfloat16)[None],
        gate_out[None],
    )


def solution(mesh):
    in_specs = (
        P("member", "fsdp", None),
        P("member", "fsdp", None),
        P("member", None, "fsdp"),
        P("member", None, "fsdp"),
        P("member", None, "fsdp"),
        P(),
        P(),
    )
    out_specs = (
        P("member", None, "fsdp"),
        P("member", None, "fsdp"),
        P("member", None, "fsdp"),
        P("member", None, "fsdp"),
    )
    shards = square_shards if mesh.shape["member"] == 4 else general_shards
    return jax.shard_map(shards, mesh=mesh, in_specs=in_specs, out_specs=out_specs, check_vma=False)
```

```python
import functools
import jax
import numpy as np
import jax.numpy as jnp
from jax import lax
from jax.experimental import pallas as pl
from jax.experimental.pallas import tpu as pltpu
from jax.sharding import PartitionSpec as P

rate_factors = (0.5, 0.8, 1.25, 2.0)
base_rate = 0.02
decay = 0.1
epsilon = 1e-08
MESH = pl.DeviceIdType.MESH
MIB = 1024 * 1024


def routes(loser, anchor):
    apart = loser ^ anchor
    if apart == 3:
        return [(anchor, anchor ^ 1, loser), (anchor, anchor ^ 2, loser)]
    other = 3 - apart
    return [(anchor, loser), (anchor, anchor ^ other, loser ^ other, loser)]


def exchange_kernel(
    loser, anchor, chunk,
    tokens, out_grad, master, first, second,
    gathered, cols, got_master, got_first, got_second,
    wide, narrow, token_send, token_recv, grad_send, grad_recv,
    state_send, state_recv, local_sem,
):
    members = lax.axis_size("member")
    ring = lax.axis_size("fsdp")
    mine = lax.axis_index("fsdp")
    member = lax.axis_index("member")
    rows = tokens.shape[1]
    width = cols.shape[1]

    barrier = pltpu.get_barrier_semaphore()
    for step in range(1, ring):
        pl.semaphore_signal(
            barrier, inc=1, device_id={"fsdp": lax.rem(mine + step, ring)}, device_id_type=MESH
        )
    for step in range(1, members):
        pl.semaphore_signal(
            barrier, inc=1, device_id={"member": lax.rem(member + step, members)}, device_id_type=MESH
        )
    pl.semaphore_wait(barrier, ring + members - 2)

    ways = routes(loser, anchor)
    depth = master.shape[1]
    pieces = depth // chunk
    split = pieces // 2 if len(ways[0]) == len(ways[1]) else pieces // 2 + 1
    spans = ((0, split), (split, pieces))
    landing = (got_first, got_second, got_master)
    starting = (first.at[0], second.at[0], narrow)

    def state_copy(kind, piece, origin, target):
        at = pl.ds(pl.multiple_of(piece * chunk, chunk), chunk)
        return pltpu.make_async_remote_copy(
            src_ref=(starting if origin else landing)[kind].at[at],
            dst_ref=landing[kind].at[at],
            send_sem=state_send.at[kind, piece],
            recv_sem=state_recv.at[kind, piece],
            device_id={"member": target},
            device_id_type=MESH,
        )

    load = pltpu.make_async_copy(master.at[0], wide, local_sem.at[0])

    @pl.when(member == anchor)
    def _():
        load.start()
        for kind in (0, 1):
            for way, (low, high) in reversed(tuple(zip(ways, spans))):
                @pl.loop(low, high)
                def _(piece):
                    state_copy(kind, piece, True, way[1]).start()

    my_rows = pl.ds(pl.multiple_of(mine * rows, rows), rows)

    def token_copy(step):
        return pltpu.make_async_remote_copy(
            src_ref=tokens.at[0],
            dst_ref=gathered.at[my_rows],
            send_sem=token_send.at[step],
            recv_sem=token_recv.at[step],
            device_id={"fsdp": lax.rem(mine + step, ring)},
            device_id_type=MESH,
        )

    def grad_copy(step):
        target = lax.rem(mine + step, ring)
        return pltpu.make_async_remote_copy(
            src_ref=out_grad.at[0, :, pl.ds(pl.multiple_of(target * width, width), width)],
            dst_ref=cols.at[my_rows],
            send_sem=grad_send.at[step],
            recv_sem=grad_recv.at[step],
            device_id={"fsdp": target},
            device_id_type=MESH,
        )

    for step in range(1, ring):
        grad_copy(step).start()
        token_copy(step).start()
    own_tokens = pltpu.make_async_copy(tokens.at[0], gathered.at[my_rows], local_sem.at[1])
    own_grad = pltpu.make_async_copy(
        out_grad.at[0, :, pl.ds(pl.multiple_of(mine * width, width), width)],
        cols.at[my_rows],
        local_sem.at[2],
    )
    own_tokens.start()
    own_grad.start()

    @pl.when(member == anchor)
    def _():
        load.wait()
        for way, (low, high) in reversed(tuple(zip(ways, spans))):
            @pl.loop(low, high)
            def _(piece):
                at = pl.ds(pl.multiple_of(piece * chunk, chunk), chunk)
                narrow[at, :] = wide[at, :].astype(narrow.dtype)
                state_copy(2, piece, True, way[1]).start()

    for way, (low, high) in zip(ways, spans):
        for here in range(1, len(way) - 1):
            @pl.when(member == way[here])
            def _():
                for kind in range(3):
                    @pl.loop(low, high)
                    def _(piece):
                        passed = state_copy(kind, piece, False, way[here + 1])
                        passed.wait_recv()
                        passed.start()

    for step in range(1, ring):
        grad_copy(step).wait()
        token_copy(step).wait()
    own_tokens.wait()
    own_grad.wait()

    for way, (low, high) in zip(ways, spans):
        @pl.when(member == way[-1])
        def _():
            for kind in range(3):
                @pl.loop(low, high)
                def _(piece):
                    state_copy(kind, piece, False, way[-2]).wait_recv()

        for here in range(len(way) - 1):
            @pl.when(member == way[here])
            def _():
                for kind in range(3):
                    @pl.loop(low, high)
                    def _(piece):
                        state_copy(kind, piece, here == 0, way[here + 1]).wait_send()


def exchange(loser, anchor, number, tokens, out_grad, master, first, second):
    ring = lax.axis_size("fsdp")
    _, rows, depth = tokens.shape
    width = master.shape[2]
    chunk = 32
    pieces = depth // chunk
    half = jax.ShapeDtypeStruct((depth, width), jnp.bfloat16)
    spot = pl.BlockSpec(memory_space=pl.ANY)
    return pl.pallas_call(
        functools.partial(exchange_kernel, loser, anchor, chunk),
        out_shape=(
            jax.ShapeDtypeStruct((ring * rows, depth), tokens.dtype),
            jax.ShapeDtypeStruct((ring * rows, width), out_grad.dtype),
            half,
            half,
            half,
        ),
        in_specs=[spot] * 5,
        out_specs=[spot] * 5,
        scratch_shapes=[
            pltpu.VMEM((depth, width), jnp.float32),
            pltpu.VMEM((depth, width), jnp.bfloat16),
            pltpu.SemaphoreType.DMA((ring,)),
            pltpu.SemaphoreType.DMA((ring,)),
            pltpu.SemaphoreType.DMA((ring,)),
            pltpu.SemaphoreType.DMA((ring,)),
            pltpu.SemaphoreType.DMA((3, pieces)),
            pltpu.SemaphoreType.DMA((3, pieces)),
            pltpu.SemaphoreType.DMA((3,)),
        ],
        compiler_params=pltpu.CompilerParams(
            collective_id=number, has_side_effects=True, vmem_limit_bytes=40 * MIB
        ),
    )(tokens, out_grad, master, first, second)


def update_kernel(
    part_rows, source, perturb, place, inputs, cols, own_master, own_first, own_second, got_master, got_first, got_second,
    new_master, new_first, new_second, gate_out, total,
):
    step = pl.program_id(0)
    is_taken = source[place[0]] != place[0]
    level = perturb[place[0]]
    rate = jnp.float32(0.0)
    for index, factor in enumerate(rate_factors):
        rate = jnp.where(level == index, np.float32(base_rate) * np.float32(factor), rate)
    block = inputs.shape[1]
    halves = []
    for low in range(0, block, part_rows):
        at = slice(low, low + part_rows)
        grad = lax.dot_general(
            inputs[:, at], cols[...], (((0,), (0,)), ((), ())), preferred_element_type=jnp.float32
        )
        weight = jnp.where(is_taken, got_master[at].astype(jnp.float32), own_master[0, at])
        first_old = jnp.where(is_taken, got_first[at], own_first[0, at]).astype(jnp.float32)
        second_old = jnp.where(is_taken, got_second[at], own_second[0, at]).astype(jnp.float32)
        first = 0.9 * first_old + 0.1 * grad
        second = 0.95 * second_old + 0.05 * grad * grad
        updated = weight - rate * (first / (jnp.sqrt(second) + epsilon) + decay * weight)
        new_master[0, at] = updated
        new_first[0, at] = first.astype(jnp.bfloat16)
        new_second[0, at] = second.astype(jnp.bfloat16)
        halves.append(updated.astype(jnp.bfloat16))
    half = jnp.concatenate(halves, axis=0)
    part = jnp.dot(inputs[...], half, preferred_element_type=jnp.float32)

    @pl.when(step == 0)
    def _():
        total[...] = part

    @pl.when(step > 0)
    def _():
        total[...] += part

    @pl.when(step == pl.num_programs(0) - 1)
    def _():
        gate_out[0] = total[...].astype(jnp.bfloat16)


def update(source, perturb, place, gathered, cols, master, first, second, got_master, got_first, got_second):
    count, depth = gathered.shape
    width = cols.shape[1]
    block, part_rows = 512, 256

    own = pl.BlockSpec(
        (1, block, width), lambda i, s, p, m: (0, jnp.where(s[m[0]] == m[0], i, 0), 0)
    )
    got = pl.BlockSpec((block, width), lambda i, s, p, m: (jnp.where(s[m[0]] == m[0], 0, i), 0))
    new = pl.BlockSpec((1, block, width), lambda i, s, p, m: (0, i, 0))
    return pl.pallas_call(
        functools.partial(update_kernel, part_rows),
        out_shape=(
            jax.ShapeDtypeStruct((1, depth, width), jnp.float32),
            jax.ShapeDtypeStruct((1, depth, width), jnp.bfloat16),
            jax.ShapeDtypeStruct((1, depth, width), jnp.bfloat16),
            jax.ShapeDtypeStruct((1, count, width), jnp.bfloat16),
        ),
        grid_spec=pltpu.PrefetchScalarGridSpec(
            num_scalar_prefetch=3,
            grid=(depth // block,),
            in_specs=[
                pl.BlockSpec((count, block), lambda i, s, p, m: (0, i)),
                pl.BlockSpec((count, width), lambda i, s, p, m: (0, 0)),
                own, own, own, got, got, got,
            ],
            out_specs=[
                new, new, new,
                pl.BlockSpec((1, count, width), lambda i, s, p, m: (0, 0, 0)),
            ],
            scratch_shapes=[pltpu.VMEM((count, width), jnp.float32)],
        ),
        compiler_params=pltpu.CompilerParams(vmem_limit_bytes=52 * MIB),
    )(source, perturb, place, gathered, cols, master, first, second, got_master, got_first, got_second)


def rate_of(perturb, member_index, positions):
    my_level = jnp.sum(jnp.where(positions == member_index, perturb, 0))
    table = jnp.array(rate_factors, dtype=jnp.float32)
    levels = jnp.arange(len(rate_factors), dtype=jnp.int32)
    return base_rate * jnp.sum(jnp.where(levels == my_level, table, 0.0))


def square_shards(tokens, out_grad, master, first_moment, second_moment, source, perturb):
    count = lax.axis_size("member")
    member_index = lax.axis_index("member")
    positions = jnp.arange(count, dtype=jnp.int32)
    pairs = [(i, j) for i in range(count) for j in range(count) if i != j]
    order = positions * (count - 1) + source - (source > positions).astype(jnp.int32)
    branch = jnp.sum(jnp.where(source != positions, order, 0))
    got = lax.switch(
        branch,
        [functools.partial(exchange, i, j, k) for k, (i, j) in enumerate(pairs)],
        tokens, out_grad, master, first_moment, second_moment,
    )
    gathered, cols, got_master, got_first, got_second = got
    return update(
        source, perturb, member_index[None], gathered, cols, master, first_moment, second_moment,
        got_master, got_first, got_second,
    )


def from_root(value, axis, source):
    kept = jnp.where(lax.axis_index(axis) == source, value, 0).astype(value.dtype)
    return lax.psum(kept, axis)


def general_shards(tokens, out_grad, master, first_moment, second_moment, source, perturb):
    count = lax.axis_size("member")
    member_index = lax.axis_index("member")
    positions = jnp.arange(count, dtype=jnp.int32)
    moments = jnp.stack([first_moment, second_moment], 1)
    losers_total = 3 * count // 8
    copying = source != positions
    earlier = positions[None, :] < positions[:, None]
    rank = jnp.sum(jnp.where(earlier & copying[None, :], 1, 0), axis=1)
    master_now = master
    moments_now = moments
    for turn in range(losers_total):
        target = jnp.sum(jnp.where(copying & (rank == turn), positions, 0))
        anchor = jnp.sum(jnp.where(positions == target, source, 0))
        got_master = from_root(master, "member", anchor)
        got_moments = from_root(moments, "member", anchor)
        taken = member_index == target
        master_now = jnp.where(taken, got_master, master_now)
        moments_now = jnp.where(taken, got_moments, moments_now)
    gathered = lax.all_gather(tokens, "fsdp", axis=1, tiled=True)
    grad_cols = lax.all_to_all(out_grad, "fsdp", split_axis=2, concat_axis=1, tiled=True)
    inputs = gathered[0]
    grad = lax.dot_general(
        inputs, grad_cols[0], (((0,), (0,)), ((), ())), preferred_element_type=jnp.float32
    )
    first = 0.9 * moments_now[0, 0].astype(jnp.float32) + 0.1 * grad
    second = 0.95 * moments_now[0, 1].astype(jnp.float32) + 0.05 * grad * grad
    rate = rate_of(perturb, member_index, positions)
    weight = master_now[0]
    updated = weight - rate * (first / (jnp.sqrt(second) + epsilon) + decay * weight)
    weight_half = updated.astype(jnp.bfloat16)
    gate_out = jnp.dot(inputs, weight_half, preferred_element_type=jnp.float32).astype(jnp.bfloat16)
    return (
        updated[None],
        first.astype(jnp.bfloat16)[None],
        second.astype(jnp.bfloat16)[None],
        gate_out[None],
    )


def solution(mesh):
    in_specs = (
        P("member", "fsdp", None),
        P("member", "fsdp", None),
        P("member", None, "fsdp"),
        P("member", None, "fsdp"),
        P("member", None, "fsdp"),
        P(),
        P(),
    )
    out_specs = (
        P("member", None, "fsdp"),
        P("member", None, "fsdp"),
        P("member", None, "fsdp"),
        P("member", None, "fsdp"),
    )
    shards = square_shards if mesh.shape["member"] == 4 else general_shards
    return jax.shard_map(shards, mesh=mesh, in_specs=in_specs, out_specs=out_specs, check_vma=False)
```
